32 devices in a mesh: wave: 32 (over z, y, x, core), lev: 1.
Axes of the slice: x: 2, y: 2, z: 4, core: 2. Of those that a mesh axis runs over, the one named last changes fastest.
Arguments:
- spectra: bfloat16 [640, 16, 2, 640], P('wave', 'lev'), may hold values from -0.3125 to 0.3125
- legendre: bfloat16 [640, 32, 640], P('wave'), may hold values from -0.25 to 0.25
- wave_slots: int32 [640], replicated, may hold values from 0 to 639, each once
- row_cycle: int32 [32], replicated, may hold values from 0 to 1279, as said below
Outputs:
- grid_fields: bfloat16 [16, 32, 6144], P(None, 'wave', 'lev')
The draws below stay inside these ranges and needn't reach their ends.
Inputs may be any that keep to these rules, and one draw needn't show every extreme that they name: `wave_slots`: each wavenumber 0 to 639 stands in exactly one slot; slot r lies on wave index r // 20. `row_cycle`: cycle numbers of distinct rows differ; cycle 0 and cycle 1280 - 1 both occur; row q lies on wave index q.
All inputs are finite; a program needn't handle non-finite values.
Results may differ from the reference program's by a relative error of at most 0.0055.
Values may be sent and summed in bfloat16 or wider, within the bound.
A program may use at most 64 MiB of HBM per device.

```python
import math
import jax
import jax.numpy as jnp
from jax import lax

DEG = 640
CYCLES = 1280
NLON = 6144
M = 640
LEVELS = 8
ROWS = 32


def draw_row_cycle(key, part):
    split_keys = jax.random.split(key)
    middle = jax.random.permutation(split_keys[0], jnp.arange(1, CYCLES - 1, dtype=jnp.int32))[:ROWS - 2]
    ending = jnp.array([0, CYCLES - 1], dtype=jnp.int32)
    joined = jnp.concatenate([middle, ending])
    return jax.random.permutation(split_keys[1], joined)


def level_of(stream_key, extent, cuts, smallest, top_value):
    def one(axis_at, shards_of):
        steps = jax.random.uniform(jax.random.fold_in(jax.random.fold_in(stream_key, 6), axis_at), (shards_of,), jnp.float32, smallest / len(cuts), top_value / len(cuts))
        return jnp.repeat(jnp.exp(steps), extent[axis_at] // shards_of).reshape((-1,) + (1,) * (len(extent) - axis_at - 1))

    level = one(*cuts[0])
    for cut in cuts[1:]:
        level = level * one(*cut)
    return level


def centred(rng, shape, scale, reach, shards=(), kind=jnp.bfloat16):
    loudness = level_of(rng, shape, shards, -0.22, 0.18) if shards else 1.0
    values = jax.random.normal(rng, shape, jnp.float32) * scale * loudness
    return jnp.minimum(jnp.maximum(values, -reach), reach).astype(kind)


def setup_inputs(seed: int = 0) -> dict:
    keys = jax.random.split(jax.random.key(seed), 5)
    spectra = centred(keys[0], (M, 2 * LEVELS, 2, DEG), (0.5 / M ** 0.5), 0.3125, ((0, 32),))
    legendre = centred(keys[1], (M, ROWS, DEG), DEG ** -0.5, 0.25, ((0, 32),))
    wave_slots = jax.random.permutation(keys[2], M).astype(jnp.int32)
    row_cycle = draw_row_cycle(jax.random.fold_in(keys[4], 71), 0)
    return dict(spectra=spectra, legendre=legendre, wave_slots=wave_slots, row_cycle=row_cycle)


two_pi = 2.0 * math.pi


def twiddle_table(slot_waves, row_points, first_col, col_count):
    columns = first_col + jnp.arange(col_count, dtype=jnp.int32)
    phase_int = (slot_waves[:, None] * columns[None, :]) % row_points
    angles = jnp.float32(two_pi) * phase_int.astype(jnp.float32) / row_points.astype(jnp.float32)
    weight = jnp.where(slot_waves == 0, jnp.float32(1.0), jnp.float32(2.0))[:, None]
    inside = (columns < row_points)[None, :]
    cosine = jnp.where(inside, weight * jnp.cos(angles), jnp.float32(0.0))
    sine_part = jnp.where(inside, -weight * jnp.sin(angles), jnp.float32(0.0))
    return jnp.concatenate([cosine, sine_part], axis=0).astype(jnp.bfloat16)


def reference(spectra, legendre, wave_slots, row_cycle):
    degree = jnp.arange(DEG, dtype=jnp.int32)
    keep_mask = degree[None, :] < (M - wave_slots)[:, None]
    masked = jnp.where(keep_mask[:, None, None, :], spectra, jnp.zeros((), spectra.dtype))

    def per_slot(inputs):
        coeffs, values = inputs
        flat_coeffs = coeffs.reshape(-1, DEG)
        return jnp.dot(flat_coeffs, values.T, preferred_element_type=jnp.float32).astype(jnp.bfloat16)

    fourier = lax.map(per_slot, (masked, legendre))
    fourier = fourier.reshape(M, 2 * LEVELS, 2, ROWS).transpose(3, 1, 2, 0).reshape(ROWS, 2 * LEVELS, 2 * M)

    def per_row(inputs):
        coeffs, cycle_number = inputs
        row_points = 20 + 4 * cycle_number
        twiddle = twiddle_table(wave_slots, row_points, 0, NLON)
        return jnp.dot(coeffs, twiddle, preferred_element_type=jnp.float32).astype(jnp.bfloat16)

    grid_rows = lax.map(per_row, (fourier, row_cycle))
    return grid_rows.transpose(1, 0, 2)
```

```python
import functools
import math

import jax
import jax.numpy as jnp
from jax import lax
from jax.experimental import pallas as pl
from jax.experimental.pallas import tpu as pltpu
from jax.sharding import PartitionSpec as P

NLON = 6144
CYCLES = 1280
BLOCK = 256
FINE = 16
NT = (((1,), (1,)), ((), ()))


def iota(shape, axis):
    return lax.broadcasted_iota(jnp.int32, shape, axis)


def sincos(waves, steps, points, inverse):
    product = waves * steps
    rest = product - jnp.round(product * inverse) * points
    half = rest * inverse * jnp.float32(math.pi)
    square = half * half
    sine = jnp.full_like(square, 1.0 / math.factorial(13))
    cosine = jnp.full_like(square, 1.0 / math.factorial(12))
    for order in (11, 9, 7, 5, 3, 1):
        sign = -1.0 if order % 4 == 3 else 1.0
        sine = sine * square + jnp.float32(sign / math.factorial(order))
        sign = -1.0 if (order - 1) % 4 == 2 else 1.0
        cosine = cosine * square + jnp.float32(sign / math.factorial(order - 1))
    sine = sine * half
    return 1.0 - 2.0 * sine * sine, 2.0 * sine * cosine


def kernel(
    waves, levs, blocks,
    slots_smem, cycle_smem, slots_ref, spectra_ref, legendre_ref, out_ref,
    spec, leg, send, recv, inner, in_sem, send_sem, recv_sem,
):
    slots_dev, pairs_dev, _, degrees = spectra_ref.shape
    rows = legendre_ref.shape[1]
    total = slots_dev * waves
    lanes = 2 * pairs_dev
    group = 128 // lanes
    groups = slots_dev // group
    devices = waves * levs
    me = lax.axis_index("wave")
    lev = lax.axis_index("lev")
    here = me * levs + lev

    def peer(step):
        there = lax.rem(here + step, devices)
        return lax.div(there, levs), lax.rem(there, levs)

    barrier = pltpu.get_barrier_semaphore()

    def greet(step, carry):
        wave_to, lev_to = peer(step)
        pl.semaphore_signal(
            barrier, inc=1, device_id={"wave": wave_to, "lev": lev_to},
            device_id_type=pl.DeviceIdType.MESH,
        )
        return carry

    loads = []
    for g in range(groups):
        part = pl.ds(g * group, group)
        loads.append((
            pltpu.make_async_copy(spectra_ref.at[part], spec.at[part], in_sem.at[0, g]),
            pltpu.make_async_copy(legendre_ref.at[part], leg.at[part], in_sem.at[1, g]),
        ))
    for pair in loads:
        for copy in pair:
            copy.start()
    lax.fori_loop(1, devices, greet, 0)

    points_int = 20 + 4 * cycle_smem[me]
    points = points_int.astype(jnp.float32)
    slots = slots_ref[...]
    slot_rows = 32
    within = iota((slot_rows, total), 1).astype(jnp.float32)
    owner = jnp.floor((within + 0.5) * jnp.float32(1.0 / slots_dev))
    is_slot = within - owner * slots_dev == iota((slot_rows, total), 0).astype(jnp.float32)
    wide = group * waves
    column = iota((wide, total), 1).astype(jnp.float32)
    column_owner = jnp.floor((column + 0.5) * jnp.float32(1.0 / slots_dev))
    wave_row = lax.rem(iota((wide, 1), 0), waves).astype(jnp.float32)
    is_owner = jnp.where(column_owner == wave_row, 1.0, 0.0).astype(jnp.bfloat16)
    ordered = jnp.zeros((slot_rows, wide), jnp.float32)
    for part, scale in ((jnp.right_shift(slots, 7), 128.0), (jnp.bitwise_and(slots, 127), 1.0)):
        chosen = jnp.where(is_slot, part.astype(jnp.float32), 0.0).astype(jnp.bfloat16)
        ordered += scale * lax.dot_general(
            chosen, is_owner, NT, preferred_element_type=jnp.float32
        )
    place = lax.div(iota((1, wide), 1), waves)
    pieces = []
    for g in range(groups):
        piece = jnp.zeros((1, wide), jnp.float32)
        for k in range(group):
            row = g * group + k
            piece = jnp.where(place == k, ordered[row : row + 1], piece)
        pieces.append(piece)
    order_waves = jnp.concatenate(pieces, axis=1)
    inverse = 1.0 / jnp.full((1, 1), points, jnp.float32)

    def table(count, stride, first):
        steps = (iota((count, total), 0) * stride + first).astype(jnp.float32)
        return sincos(order_waves, steps, points, inverse)

    degree = iota((1, degrees), 1)
    lane_slot = lax.div(iota((rows, 128), 1), lanes)
    for g in range(groups):
        for copy in loads[g]:
            copy.wait()
        kept = []
        for k in range(group):
            r = g * group + k
            limit = total - slots_smem[me * slots_dev + r]
            keep = jnp.where(degree < limit, 1.0, 0.0).astype(jnp.bfloat16)
            kept.append(spec[r].reshape(lanes, degrees) * keep)
        values = leg[pl.ds(g * group, group)].reshape(group * rows, degrees)
        product = lax.dot_general(
            values, jnp.concatenate(kept, axis=0), NT, preferred_element_type=jnp.float32
        )
        fourier = product[:rows]
        for k in range(1, group):
            fourier = jnp.where(lane_slot == k, product[k * rows : (k + 1) * rows], fourier)
        fourier = fourier.astype(jnp.bfloat16).astype(jnp.float32)
        send[:, :, pl.ds(g * 128, 128)] = fourier.reshape(rows, 1, 128)

    slot_here = lev * waves + me
    pl.semaphore_wait(barrier, devices - 1)

    def deliver(step, carry):
        wave_to, lev_to = peer(step)
        pltpu.make_async_remote_copy(
            src_ref=send.at[wave_to], dst_ref=recv.at[slot_here],
            send_sem=send_sem, recv_sem=recv_sem,
            device_id={"wave": wave_to, "lev": lev_to}, device_id_type=pl.DeviceIdType.MESH,
        ).start()
        return carry

    lax.fori_loop(1, devices, deliver, 0)
    recv[slot_here] = send[me]

    first = lev * (NLON // levs)
    coarse_cos, coarse_sin = table(BLOCK // FINE, FINE, 0)
    fine_cos, fine_sin = table(FINE, 1, 0)
    for a in range(BLOCK // FINE):
        ca, sa = coarse_cos[a : a + 1], coarse_sin[a : a + 1]
        inner[a * FINE : (a + 1) * FINE, :total] = (ca * fine_cos - sa * fine_sin).astype(jnp.bfloat16)
        inner[a * FINE : (a + 1) * FINE, total:] = (-(sa * fine_cos + ca * fine_sin)).astype(jnp.bfloat16)
    outer_cos, outer_sin = table(-(-blocks // 8) * 8, BLOCK, first)
    weight = jnp.where(order_waves == 0.0, 1.0, 2.0)
    pick_row = iota((lanes, 128), 0)
    pick_pair = jnp.where(pick_row < pairs_dev, 2 * pick_row, 2 * (pick_row - pairs_dev) + 1)
    pick = jnp.where(lax.rem(iota((lanes, 128), 1), lanes) == pick_pair, 1.0, 0.0).astype(jnp.bfloat16)
    arrived_slot = lax.div(iota((waves, 128), 1), lanes)

    for sem in (recv_sem, send_sem):
        all_of_them = recv.at[pl.ds(0, devices - 1)]
        pltpu.make_async_copy(all_of_them, all_of_them, sem).wait()

    reals, imags = [], []
    for v in range(levs):
        parts = []
        for g in range(groups):
            block = recv[v * waves : (v + 1) * waves, :, pl.ds(g * 128, 128)].reshape(waves, 128)
            spread = jnp.concatenate(
                [jnp.where(arrived_slot == k, block, 0.0) for k in range(group)], axis=0
            ).astype(jnp.bfloat16)
            parts.append(lax.dot_general(pick, spread, NT, preferred_element_type=jnp.float32))
        coeffs = jnp.concatenate(parts, axis=1) * weight
        reals.append(coeffs[:pairs_dev])
        imags.append(coeffs[pairs_dev:])
    real = jnp.concatenate(reals, axis=0)
    imag = jnp.concatenate(imags, axis=0)
    pairs = real.shape[0]

    at = iota((pairs, BLOCK), 1) + first
    step = 7 if blocks % 7 == 0 else 2
    for start in range(0, blocks, step):
        turned = []
        for j in range(start, start + step):
            c, s = outer_cos[j : j + 1], outer_sin[j : j + 1]
            turned.append(jnp.concatenate(
                [(real * c - imag * s).astype(jnp.bfloat16), (real * s + imag * c).astype(jnp.bfloat16)],
                axis=1,
            ))
        result = lax.dot_general(
            jnp.concatenate(turned, axis=0), inner[...], NT, preferred_element_type=jnp.float32
        )
        for j in range(start, start + step):
            found = result[(j - start) * pairs : (j - start + 1) * pairs]
            found = jnp.where(at + j * BLOCK < points_int, found, 0.0)
            out_ref[:, j * BLOCK : (j + 1) * BLOCK] = found.astype(jnp.bfloat16)
    if blocks * BLOCK < out_ref.shape[1]:
        rest = out_ref.shape[1] - blocks * BLOCK
        out_ref[:, blocks * BLOCK :] = jnp.zeros((pairs, rest), jnp.bfloat16)


def shards(spectra, legendre, wave_slots, row_cycle):
    waves = lax.axis_size("wave")
    levs = lax.axis_size("lev")
    slots_dev, pairs_dev, _, degrees = spectra.shape
    rows = legendre.shape[1]
    total = slots_dev * waves
    region = NLON // levs
    blocks = min(region // BLOCK, -(-(20 + 4 * (CYCLES - 1)) // BLOCK))
    width = slots_dev * 2 * pairs_dev
    smem = pl.BlockSpec(memory_space=pltpu.SMEM)
    vmem = pl.BlockSpec(memory_space=pltpu.VMEM)
    hbm = pl.BlockSpec(memory_space=pl.ANY)
    grid = pl.pallas_call(
        functools.partial(kernel, waves, levs, blocks),
        out_shape=jax.ShapeDtypeStruct((pairs_dev * levs, region), jnp.bfloat16),
        in_specs=[smem, smem, vmem, hbm, hbm],
        out_specs=vmem,
        scratch_shapes=[
            pltpu.VMEM((slots_dev, pairs_dev, 2, degrees), jnp.bfloat16),
            pltpu.VMEM((slots_dev, rows, degrees), jnp.bfloat16),
            pltpu.VMEM((rows, 1, width), jnp.float32),
            pltpu.VMEM((levs * waves, 1, width), jnp.float32),
            pltpu.VMEM((BLOCK, 2 * total), jnp.bfloat16),
            pltpu.SemaphoreType.DMA((2, slots_dev * 2 * pairs_dev // 128)),
            pltpu.SemaphoreType.DMA,
            pltpu.SemaphoreType.DMA,
        ],
        compiler_params=pltpu.CompilerParams(
            collective_id=0, has_side_effects=True, vmem_limit_bytes=48 << 20
        ),
    )(wave_slots, row_cycle, wave_slots.reshape(1, total), spectra, legendre)
    return grid.reshape(grid.shape[0], 1, region)


def solution(mesh):
    placed = (P("wave", "lev", None, None), P("wave", None, None), P(), P())
    return jax.shard_map(
        shards, mesh=mesh, in_specs=placed, out_specs=P(None, "wave", "lev"), check_vma=False
    )
```

```python
import functools
import math

import jax
import jax.numpy as jnp
from jax import lax
from jax.experimental import pallas as pl
from jax.experimental.pallas import tpu as pltpu
from jax.sharding import PartitionSpec as P

NLON = 6144
CYCLES = 1280
BLOCK = 256
FINE = 16
NT = (((1,), (1,)), ((), ()))


def iota(shape, axis):
    return lax.broadcasted_iota(jnp.int32, shape, axis)


def sincos(waves, steps, points, inverse):
    product = waves * steps
    rest = product - jnp.round(product * inverse) * points
    half = rest * inverse * jnp.float32(math.pi)
    square = half * half
    sine = jnp.full_like(square, 1.0 / math.factorial(13))
    cosine = jnp.full_like(square, 1.0 / math.factorial(12))
    for order in (11, 9, 7, 5, 3, 1):
        sign = -1.0 if order % 4 == 3 else 1.0
        sine = sine * square + jnp.float32(sign / math.factorial(order))
        sign = -1.0 if (order - 1) % 4 == 2 else 1.0
        cosine = cosine * square + jnp.float32(sign / math.factorial(order - 1))
    sine = sine * half
    return 1.0 - 2.0 * sine * sine, 2.0 * sine * cosine


def kernel(
    waves, levs, blocks,
    slots_ref, cycle_ref, spectra_ref, legendre_ref, out_ref,
    slots_smem, cycle_smem, slots_vmem, spec, leg, send, recv, inner,
    small_sem, in_sem, send_sem, recv_sem,
):
    slots_dev, pairs_dev, _, degrees = spectra_ref.shape
    rows = legendre_ref.shape[1]
    total = slots_dev * waves
    lanes = 2 * pairs_dev
    group = 128 // lanes
    groups = slots_dev // group
    devices = waves * levs
    me = lax.axis_index("wave")
    lev = lax.axis_index("lev")
    here = me * levs + lev

    def peer(step):
        there = lax.rem(here + step, devices)
        return lax.div(there, levs), lax.rem(there, levs)

    barrier = pltpu.get_barrier_semaphore()

    def greet(step, carry):
        wave_to, lev_to = peer(step)
        pl.semaphore_signal(
            barrier, inc=1, device_id={"wave": wave_to, "lev": lev_to},
            device_id_type=pl.DeviceIdType.MESH,
        )
        return carry

    small = [
        pltpu.make_async_copy(slots_ref, slots_vmem, small_sem.at[0]),
        pltpu.make_async_copy(cycle_ref, cycle_smem, small_sem.at[1]),
        pltpu.make_async_copy(slots_ref, slots_smem, small_sem.at[2]),
    ]
    for copy in small:
        copy.start()
    loads = []
    for g in range(groups):
        part = pl.ds(g * group, group)
        loads.append((
            pltpu.make_async_copy(spectra_ref.at[part], spec.at[part], in_sem.at[0, g]),
            pltpu.make_async_copy(legendre_ref.at[part], leg.at[part], in_sem.at[1, g]),
        ))
    for pair in loads:
        for copy in pair:
            copy.start()
    lax.fori_loop(1, devices, greet, 0)

    for copy in small:
        copy.wait()
    points_int = 20 + 4 * cycle_smem[me]
    points = points_int.astype(jnp.float32)
    slots = slots_vmem[...].reshape(1, total)
    slot_rows = 32
    within = iota((slot_rows, total), 1).astype(jnp.float32)
    owner = jnp.floor((within + 0.5) * jnp.float32(1.0 / slots_dev))
    is_slot = within - owner * slots_dev == iota((slot_rows, total), 0).astype(jnp.float32)
    wide = group * waves
    column = iota((wide, total), 1).astype(jnp.float32)
    column_owner = jnp.floor((column + 0.5) * jnp.float32(1.0 / slots_dev))
    wave_row = lax.rem(iota((wide, 1), 0), waves).astype(jnp.float32)
    is_owner = jnp.where(column_owner == wave_row, 1.0, 0.0).astype(jnp.bfloat16)
    ordered = jnp.zeros((slot_rows, wide), jnp.float32)
    for part, scale in ((jnp.right_shift(slots, 7), 128.0), (jnp.bitwise_and(slots, 127), 1.0)):
        chosen = jnp.where(is_slot, part.astype(jnp.float32), 0.0).astype(jnp.bfloat16)
        ordered += scale * lax.dot_general(
            chosen, is_owner, NT, preferred_element_type=jnp.float32
        )
    place = lax.div(iota((1, wide), 1), waves)
    pieces = []
    for g in range(groups):
        piece = jnp.zeros((1, wide), jnp.float32)
        for k in range(group):
            row = g * group + k
            piece = jnp.where(place == k, ordered[row : row + 1], piece)
        pieces.append(piece)
    order_waves = jnp.concatenate(pieces, axis=1)
    inverse = 1.0 / jnp.full((1, 1), points, jnp.float32)

    def table(count, stride, first):
        steps = (iota((count, total), 0) * stride + first).astype(jnp.float32)
        return sincos(order_waves, steps, points, inverse)

    degree = iota((1, degrees), 1)
    lane_slot = lax.div(iota((rows, 128), 1), lanes)
    for g in range(groups):
        for copy in loads[g]:
            copy.wait()
        kept = []
        for k in range(group):
            r = g * group + k
            limit = total - slots_smem[me * slots_dev + r]
            keep = jnp.where(degree < limit, 1.0, 0.0).astype(jnp.bfloat16)
            kept.append(spec[r].reshape(lanes, degrees) * keep)
        values = leg[pl.ds(g * group, group)].reshape(group * rows, degrees)
        product = lax.dot_general(
            values, jnp.concatenate(kept, axis=0), NT, preferred_element_type=jnp.float32
        )
        fourier = product[:rows]
        for k in range(1, group):
            fourier = jnp.where(lane_slot == k, product[k * rows : (k + 1) * rows], fourier)
        fourier = fourier.astype(jnp.bfloat16).astype(jnp.float32)
        send[:, :, pl.ds(g * 128, 128)] = fourier.reshape(rows, 1, 128)

    slot_here = lev * waves + me
    pl.semaphore_wait(barrier, devices - 1)

    def deliver(step, carry):
        wave_to, lev_to = peer(step)
        pltpu.make_async_remote_copy(
            src_ref=send.at[wave_to], dst_ref=recv.at[slot_here],
            send_sem=send_sem, recv_sem=recv_sem,
            device_id={"wave": wave_to, "lev": lev_to}, device_id_type=pl.DeviceIdType.MESH,
        ).start()
        return carry

    lax.fori_loop(1, devices, deliver, 0)
    recv[slot_here] = send[me]

    first = lev * (NLON // levs)
    coarse_cos, coarse_sin = table(BLOCK // FINE, FINE, 0)
    fine_cos, fine_sin = table(FINE, 1, 0)
    for a in range(BLOCK // FINE):
        ca, sa = coarse_cos[a : a + 1], coarse_sin[a : a + 1]
        inner[a * FINE : (a + 1) * FINE, :total] = (ca * fine_cos - sa * fine_sin).astype(jnp.bfloat16)
        inner[a * FINE : (a + 1) * FINE, total:] = (-(sa * fine_cos + ca * fine_sin)).astype(jnp.bfloat16)
    outer_cos, outer_sin = table(-(-blocks // 8) * 8, BLOCK, first)
    weight = jnp.where(order_waves == 0.0, 1.0, 2.0)
    pick_row = iota((lanes, 128), 0)
    pick_pair = jnp.where(pick_row < pairs_dev, 2 * pick_row, 2 * (pick_row - pairs_dev) + 1)
    pick = jnp.where(lax.rem(iota((lanes, 128), 1), lanes) == pick_pair, 1.0, 0.0).astype(jnp.bfloat16)
    arrived_slot = lax.div(iota((waves, 128), 1), lanes)

    for sem in (recv_sem, send_sem):
        all_of_them = recv.at[pl.ds(0, devices - 1)]
        pltpu.make_async_copy(all_of_them, all_of_them, sem).wait()

    reals, imags = [], []
    for v in range(levs):
        parts = []
        for g in range(groups):
            block = recv[v * waves : (v + 1) * waves, :, pl.ds(g * 128, 128)].reshape(waves, 128)
            spread = jnp.concatenate(
                [jnp.where(arrived_slot == k, block, 0.0) for k in range(group)], axis=0
            ).astype(jnp.bfloat16)
            parts.append(lax.dot_general(pick, spread, NT, preferred_element_type=jnp.float32))
        coeffs = jnp.concatenate(parts, axis=1) * weight
        reals.append(coeffs[:pairs_dev])
        imags.append(coeffs[pairs_dev:])
    real = jnp.concatenate(reals, axis=0)
    imag = jnp.concatenate(imags, axis=0)
    pairs = real.shape[0]

    at = iota((pairs, BLOCK), 1) + first
    step = 7 if blocks % 7 == 0 else 2
    for start in range(0, blocks, step):
        turned = []
        for j in range(start, start + step):
            c, s = outer_cos[j : j + 1], outer_sin[j : j + 1]
            turned.append(jnp.concatenate(
                [(real * c - imag * s).astype(jnp.bfloat16), (real * s + imag * c).astype(jnp.bfloat16)],
                axis=1,
            ))
        result = lax.dot_general(
            jnp.concatenate(turned, axis=0), inner[...], NT, preferred_element_type=jnp.float32
        )
        for j in range(start, start + step):
            found = result[(j - start) * pairs : (j - start + 1) * pairs]
            found = jnp.where(at + j * BLOCK < points_int, found, 0.0)
            out_ref[:, j * BLOCK : (j + 1) * BLOCK] = found.astype(jnp.bfloat16)
    if blocks * BLOCK < out_ref.shape[1]:
        rest = out_ref.shape[1] - blocks * BLOCK
        out_ref[:, blocks * BLOCK :] = jnp.zeros((pairs, rest), jnp.bfloat16)


def shards(spectra, legendre, wave_slots, row_cycle):
    waves = lax.axis_size("wave")
    levs = lax.axis_size("lev")
    slots_dev, pairs_dev, _, degrees = spectra.shape
    rows = legendre.shape[1]
    total = slots_dev * waves
    region = NLON // levs
    blocks = min(region // BLOCK, -(-(20 + 4 * (CYCLES - 1)) // BLOCK))
    width = slots_dev * 2 * pairs_dev
    vmem = pl.BlockSpec(memory_space=pltpu.VMEM)
    hbm = pl.BlockSpec(memory_space=pltpu.HBM)
    grid = pl.pallas_call(
        functools.partial(kernel, waves, levs, blocks),
        out_shape=pltpu.VMEM((pairs_dev * levs, region), jnp.bfloat16),
        in_specs=[hbm] * 4,
        out_specs=vmem,
        scratch_shapes=[
            pltpu.SMEM((total,), jnp.int32),
            pltpu.SMEM((waves,), jnp.int32),
            pltpu.VMEM((total,), jnp.int32),
            pltpu.VMEM((slots_dev, pairs_dev, 2, degrees), jnp.bfloat16),
            pltpu.VMEM((slots_dev, rows, degrees), jnp.bfloat16),
            pltpu.VMEM((rows, 1, width), jnp.float32),
            pltpu.VMEM((levs * waves, 1, width), jnp.float32),
            pltpu.VMEM((BLOCK, 2 * total), jnp.bfloat16),
            pltpu.SemaphoreType.DMA((3,)),
            pltpu.SemaphoreType.DMA((2, slots_dev * 2 * pairs_dev // 128)),
            pltpu.SemaphoreType.DMA,
            pltpu.SemaphoreType.DMA,
        ],
        compiler_params=pltpu.CompilerParams(
            collective_id=0, has_side_effects=True, vmem_limit_bytes=60 << 20
        ),
    )(wave_slots, row_cycle, spectra, legendre)
    return grid.reshape(grid.shape[0], 1, region)


def solution(mesh):
    placed = (P("wave", "lev", None, None), P("wave", None, None), P(), P())
    return jax.shard_map(
        shards, mesh=mesh, in_specs=placed, out_specs=P(None, "wave", "lev"), check_vma=False
    )
```

```python
import functools
import math

import jax
import jax.numpy as jnp
from jax import lax
from jax.experimental import pallas as pl
from jax.experimental.pallas import tpu as pltpu
from jax.sharding import PartitionSpec as P

NLON = 6144
CYCLES = 1280
BLOCK = 256
FINE = 16
NT = (((1,), (1,)), ((), ()))


def iota(shape, axis):
    return lax.broadcasted_iota(jnp.int32, shape, axis)


def sincos(waves, steps, points, inverse):
    product = waves * steps
    rest = product - jnp.round(product * inverse) * points
    half = rest * inverse * jnp.float32(math.pi)
    square = half * half
    sine = jnp.full_like(square, 1.0 / math.factorial(13))
    cosine = jnp.full_like(square, 1.0 / math.factorial(12))
    for order in (11, 9, 7, 5, 3, 1):
        sign = -1.0 if order % 4 == 3 else 1.0
        sine = sine * square + jnp.float32(sign / math.factorial(order))
        sign = -1.0 if (order - 1) % 4 == 2 else 1.0
        cosine = cosine * square + jnp.float32(sign / math.factorial(order - 1))
    sine = sine * half
    return 1.0 - 2.0 * sine * sine, 2.0 * sine * cosine


def kernel(
    waves, levs, blocks,
    slots_ref, cycle_ref, spectra_ref, legendre_ref, out_ref,
    slots_smem, cycle_smem, slots_vmem, spec, leg, send, recv, inner,
    small_sem, in_sem, send_sem, recv_sem,
):
    slots_dev, pairs_dev, _, degrees = spectra_ref.shape
    rows = legendre_ref.shape[1]
    total = slots_dev * waves
    lanes = 2 * pairs_dev
    group = 128 // lanes
    groups = slots_dev // group
    devices = waves * levs
    me = lax.axis_index("wave")
    lev = lax.axis_index("lev")
    here = me * levs + lev

    def peer(step):
        there = lax.rem(here + step, devices)
        return lax.div(there, levs), lax.rem(there, levs)

    barrier = pltpu.get_barrier_semaphore()

    def greet(step, carry):
        wave_to, lev_to = peer(step)
        pl.semaphore_signal(
            barrier, inc=1, device_id={"wave": wave_to, "lev": lev_to},
            device_id_type=pl.DeviceIdType.MESH,
        )
        return carry

    small = [
        pltpu.make_async_copy(slots_ref, slots_vmem, small_sem.at[0]),
        pltpu.make_async_copy(cycle_ref, cycle_smem, small_sem.at[1]),
        pltpu.make_async_copy(slots_ref, slots_smem, small_sem.at[2]),
    ]
    for copy in small:
        copy.start()
    loads = []
    for g in range(1):
        part = pl.ds(0, slots_dev)
        loads.append((
            pltpu.make_async_copy(spectra_ref.at[part], spec.at[part], in_sem.at[0, g]),
            pltpu.make_async_copy(legendre_ref.at[part], leg.at[part], in_sem.at[1, g]),
        ))
    for pair in loads:
        for copy in pair:
            copy.start()
    lax.fori_loop(1, devices, greet, 0)

    small[2].wait()
    degree = iota((1, degrees), 1)
    lane_slot = lax.div(iota((rows, 128), 1), lanes)
    for g in range(groups):
        for copy in loads[0] if g == 0 else ():
            copy.wait()
        kept = []
        for k in range(group):
            r = g * group + k
            limit = total - slots_smem[me * slots_dev + r]
            keep = jnp.where(degree < limit, 1.0, 0.0).astype(jnp.bfloat16)
            kept.append(spec[r].reshape(lanes, degrees) * keep)
        values = leg[pl.ds(g * group, group)].reshape(group * rows, degrees)
        product = lax.dot_general(
            values, jnp.concatenate(kept, axis=0), NT, preferred_element_type=jnp.float32
        )
        fourier = product[:rows]
        for k in range(1, group):
            fourier = jnp.where(lane_slot == k, product[k * rows : (k + 1) * rows], fourier)
        fourier = fourier.astype(jnp.bfloat16).astype(jnp.float32)
        send[:, :, pl.ds(g * 128, 128)] = fourier.reshape(rows, 1, 128)

    slot_here = lev * waves + me
    pl.semaphore_wait(barrier, devices - 1)

    def deliver(step, carry):
        wave_to, lev_to = peer(step)
        pltpu.make_async_remote_copy(
            src_ref=send.at[wave_to], dst_ref=recv.at[slot_here],
            send_sem=send_sem, recv_sem=recv_sem,
            device_id={"wave": wave_to, "lev": lev_to}, device_id_type=pl.DeviceIdType.MESH,
        ).start()
        return carry

    lax.fori_loop(1, devices, deliver, 0)
    recv[slot_here] = send[me]

    small[0].wait()
    small[1].wait()
    points_int = 20 + 4 * cycle_smem[me]
    points = points_int.astype(jnp.float32)
    slots = slots_vmem[...].reshape(1, total)
    slot_rows = 32
    within = iota((slot_rows, total), 1).astype(jnp.float32)
    owner = jnp.floor((within + 0.5) * jnp.float32(1.0 / slots_dev))
    is_slot = within - owner * slots_dev == iota((slot_rows, total), 0).astype(jnp.float32)
    wide = group * waves
    column = iota((wide, total), 1).astype(jnp.float32)
    column_owner = jnp.floor((column + 0.5) * jnp.float32(1.0 / slots_dev))
    wave_row = lax.rem(iota((wide, 1), 0), waves).astype(jnp.float32)
    is_owner = jnp.where(column_owner == wave_row, 1.0, 0.0).astype(jnp.bfloat16)
    ordered = jnp.zeros((slot_rows, wide), jnp.float32)
    for part, scale in ((jnp.right_shift(slots, 7), 128.0), (jnp.bitwise_and(slots, 127), 1.0)):
        chosen = jnp.where(is_slot, part.astype(jnp.float32), 0.0).astype(jnp.bfloat16)
        ordered += scale * lax.dot_general(
            chosen, is_owner, NT, preferred_element_type=jnp.float32
        )
    place = lax.div(iota((1, wide), 1), waves)
    pieces = []
    for g in range(groups):
        piece = jnp.zeros((1, wide), jnp.float32)
        for k in range(group):
            row = g * group + k
            piece = jnp.where(place == k, ordered[row : row + 1], piece)
        pieces.append(piece)
    order_waves = jnp.concatenate(pieces, axis=1)
    inverse = 1.0 / jnp.full((1, 1), points, jnp.float32)

    def table(count, stride, first):
        steps = (iota((count, total), 0) * stride + first).astype(jnp.float32)
        return sincos(order_waves, steps, points, inverse)

    first = lev * (NLON // levs)
    coarse_cos, coarse_sin = table(BLOCK // FINE, FINE, 0)
    fine_cos, fine_sin = table(FINE, 1, 0)
    for a in range(BLOCK // FINE):
        ca, sa = coarse_cos[a : a + 1], coarse_sin[a : a + 1]
        inner[a * FINE : (a + 1) * FINE, :total] = (ca * fine_cos - sa * fine_sin).astype(jnp.bfloat16)
        inner[a * FINE : (a + 1) * FINE, total:] = (-(sa * fine_cos + ca * fine_sin)).astype(jnp.bfloat16)
    outer_cos, outer_sin = table(-(-blocks // 8) * 8, BLOCK, first)
    weight = jnp.where(order_waves == 0.0, 1.0, 2.0)
    pick_row = iota((lanes, 128), 0)
    pick_pair = jnp.where(pick_row < pairs_dev, 2 * pick_row, 2 * (pick_row - pairs_dev) + 1)
    pick = jnp.where(lax.rem(iota((lanes, 128), 1), lanes) == pick_pair, 1.0, 0.0).astype(jnp.bfloat16)
    arrived_slot = lax.div(iota((waves, 128), 1), lanes)

    for sem in (recv_sem, send_sem):
        all_of_them = recv.at[pl.ds(0, devices - 1)]
        pltpu.make_async_copy(all_of_them, all_of_them, sem).wait()

    reals, imags = [], []
    for v in range(levs):
        parts = []
        for g in range(groups):
            block = recv[v * waves : (v + 1) * waves, :, pl.ds(g * 128, 128)].reshape(waves, 128)
            spread = jnp.concatenate(
                [jnp.where(arrived_slot == k, block, 0.0) for k in range(group)], axis=0
            ).astype(jnp.bfloat16)
            parts.append(lax.dot_general(pick, spread, NT, preferred_element_type=jnp.float32))
        coeffs = jnp.concatenate(parts, axis=1) * weight
        reals.append(coeffs[:pairs_dev])
        imags.append(coeffs[pairs_dev:])
    real = jnp.concatenate(reals, axis=0)
    imag = jnp.concatenate(imags, axis=0)
    pairs = real.shape[0]

    at = iota((pairs, BLOCK), 1) + first
    step = 7 if blocks % 7 == 0 else 2
    for start in range(0, blocks, step):
        turned = []
        for j in range(start, start + step):
            c, s = outer_cos[j : j + 1], outer_sin[j : j + 1]
            turned.append(jnp.concatenate(
                [(real * c - imag * s).astype(jnp.bfloat16), (real * s + imag * c).astype(jnp.bfloat16)],
                axis=1,
            ))
        result = lax.dot_general(
            jnp.concatenate(turned, axis=0), inner[...], NT, preferred_element_type=jnp.float32
        )
        for j in range(start, start + step):
            found = result[(j - start) * pairs : (j - start + 1) * pairs]
            found = jnp.where(at + j * BLOCK < points_int, found, 0.0)
            out_ref[:, j * BLOCK : (j + 1) * BLOCK] = found.astype(jnp.bfloat16)
    if blocks * BLOCK < out_ref.shape[1]:
        rest = out_ref.shape[1] - blocks * BLOCK
        out_ref[:, blocks * BLOCK :] = jnp.zeros((pairs, rest), jnp.bfloat16)


def shards(spectra, legendre, wave_slots, row_cycle):
    waves = lax.axis_size("wave")
    levs = lax.axis_size("lev")
    slots_dev, pairs_dev, _, degrees = spectra.shape
    rows = legendre.shape[1]
    total = slots_dev * waves
    region = NLON // levs
    blocks = min(region // BLOCK, -(-(20 + 4 * (CYCLES - 1)) // BLOCK))
    width = slots_dev * 2 * pairs_dev
    vmem = pl.BlockSpec(memory_space=pltpu.VMEM)
    hbm = pl.BlockSpec(memory_space=pltpu.HBM)
    grid = pl.pallas_call(
        functools.partial(kernel, waves, levs, blocks),
        out_shape=pltpu.VMEM((pairs_dev * levs, region), jnp.bfloat16),
        in_specs=[hbm] * 4,
        out_specs=vmem,
        scratch_shapes=[
            pltpu.SMEM((total,), jnp.int32),
            pltpu.SMEM((waves,), jnp.int32),
            pltpu.VMEM((total,), jnp.int32),
            pltpu.VMEM((slots_dev, pairs_dev, 2, degrees), jnp.bfloat16),
            pltpu.VMEM((slots_dev, rows, degrees), jnp.bfloat16),
            pltpu.VMEM((rows, 1, width), jnp.float32),
            pltpu.VMEM((levs * waves, 1, width), jnp.float32),
            pltpu.VMEM((BLOCK, 2 * total), jnp.bfloat16),
            pltpu.SemaphoreType.DMA((3,)),
            pltpu.SemaphoreType.DMA((2, slots_dev * 2 * pairs_dev // 128)),
            pltpu.SemaphoreType.DMA,
            pltpu.SemaphoreType.DMA,
        ],
        compiler_params=pltpu.CompilerParams(
            collective_id=0, has_side_effects=True, vmem_limit_bytes=60 << 20
        ),
    )(wave_slots, row_cycle, spectra, legendre)
    return grid.reshape(grid.shape[0], 1, region)


def solution(mesh):
    placed = (P("wave", "lev", None, None), P("wave", None, None), P(), P())
    return jax.shard_map(
        shards, mesh=mesh, in_specs=placed, out_specs=P(None, "wave", "lev"), check_vma=False
    )
```

```python
import functools
import math

import jax
import jax.numpy as jnp
from jax import lax
from jax.experimental import pallas as pl
from jax.experimental.pallas import tpu as pltpu
from jax.sharding import PartitionSpec as P

NLON = 6144
CYCLES = 1280
BLOCK = 256
FINE = 16
NT = (((1,), (1,)), ((), ()))


def iota(shape, axis):
    return lax.broadcasted_iota(jnp.int32, shape, axis)


def sincos(waves, steps, points, inverse):
    product = waves * steps
    rest = product - jnp.round(product * inverse) * points
    half = rest * inverse * jnp.float32(math.pi)
    square = half * half
    sine = jnp.full_like(square, 1.0 / math.factorial(13))
    cosine = jnp.full_like(square, 1.0 / math.factorial(12))
    for order in (11, 9, 7, 5, 3, 1):
        sign = -1.0 if order % 4 == 3 else 1.0
        sine = sine * square + jnp.float32(sign / math.factorial(order))
        sign = -1.0 if (order - 1) % 4 == 2 else 1.0
        cosine = cosine * square + jnp.float32(sign / math.factorial(order - 1))
    sine = sine * half
    return 1.0 - 2.0 * sine * sine, 2.0 * sine * cosine


def kernel(
    waves, levs, blocks,
    slots_ref, cycle_ref, spectra_ref, legendre_ref, out_ref,
    slots_smem, cycle_smem, slots_vmem, spec, leg, send, recv, inner,
    small_sem, in_sem, send_sem, recv_sem,
):
    slots_dev, pairs_dev, _, degrees = spectra_ref.shape
    rows = legendre_ref.shape[1]
    total = slots_dev * waves
    lanes = 2 * pairs_dev
    group = 128 // lanes
    groups = slots_dev // group
    devices = waves * levs
    me = lax.axis_index("wave")
    lev = lax.axis_index("lev")
    here = me * levs + lev

    def peer(step):
        there = lax.rem(here + step, devices)
        return lax.div(there, levs), lax.rem(there, levs)

    barrier = pltpu.get_barrier_semaphore()

    def greet(step, carry):
        wave_to, lev_to = peer(step)
        pl.semaphore_signal(
            barrier, inc=1, device_id={"wave": wave_to, "lev": lev_to},
            device_id_type=pl.DeviceIdType.MESH,
        )
        return carry

    small = [
        pltpu.make_async_copy(slots_ref, slots_vmem, small_sem.at[0]),
        pltpu.make_async_copy(cycle_ref, cycle_smem, small_sem.at[1]),
        pltpu.make_async_copy(slots_ref, slots_smem, small_sem.at[2]),
    ]
    for copy in small:
        copy.start()
    loads = []
    half = groups // 2 * group
    for g, part in ((0, pl.ds(0, half)), (1, pl.ds(half, slots_dev - half))):
        loads.append((
            pltpu.make_async_copy(spectra_ref.at[part], spec.at[part], in_sem.at[0, g]),
            pltpu.make_async_copy(legendre_ref.at[part], leg.at[part], in_sem.at[1, g]),
        ))
    for pair in loads:
        for copy in pair:
            copy.start()
    lax.fori_loop(1, devices, greet, 0)

    small[2].wait()
    degree = iota((1, degrees), 1)
    lane_slot = lax.div(iota((rows, 128), 1), lanes)
    for g in range(groups):
        for copy in loads[0] if g == 0 else loads[1] if g == groups // 2 else ():
            copy.wait()
        kept = []
        for k in range(group):
            r = g * group + k
            limit = total - slots_smem[me * slots_dev + r]
            keep = jnp.where(degree < limit, 1.0, 0.0).astype(jnp.bfloat16)
            kept.append(spec[r].reshape(lanes, degrees) * keep)
        values = leg[pl.ds(g * group, group)].reshape(group * rows, degrees)
        product = lax.dot_general(
            values, jnp.concatenate(kept, axis=0), NT, preferred_element_type=jnp.float32
        )
        fourier = product[:rows]
        for k in range(1, group):
            fourier = jnp.where(lane_slot == k, product[k * rows : (k + 1) * rows], fourier)
        fourier = fourier.astype(jnp.bfloat16).astype(jnp.float32)
        send[:, :, pl.ds(g * 128, 128)] = fourier.reshape(rows, 1, 128)

    slot_here = lev * waves + me
    pl.semaphore_wait(barrier, devices - 1)

    def deliver(step, carry):
        wave_to, lev_to = peer(step)
        pltpu.make_async_remote_copy(
            src_ref=send.at[wave_to], dst_ref=recv.at[slot_here],
            send_sem=send_sem, recv_sem=recv_sem,
            device_id={"wave": wave_to, "lev": lev_to}, device_id_type=pl.DeviceIdType.MESH,
        ).start()
        return carry

    lax.fori_loop(1, devices, deliver, 0)
    recv[slot_here] = send[me]

    small[0].wait()
    small[1].wait()
    points_int = 20 + 4 * cycle_smem[me]
    points = points_int.astype(jnp.float32)
    slots = slots_vmem[...].reshape(1, total)
    slot_rows = 32
    within = iota((slot_rows, total), 1).astype(jnp.float32)
    owner = jnp.floor((within + 0.5) * jnp.float32(1.0 / slots_dev))
    is_slot = within - owner * slots_dev == iota((slot_rows, total), 0).astype(jnp.float32)
    wide = group * waves
    column = iota((wide, total), 1).astype(jnp.float32)
    column_owner = jnp.floor((column + 0.5) * jnp.float32(1.0 / slots_dev))
    wave_row = lax.rem(iota((wide, 1), 0), waves).astype(jnp.float32)
    is_owner = jnp.where(column_owner == wave_row, 1.0, 0.0).astype(jnp.bfloat16)
    ordered = jnp.zeros((slot_rows, wide), jnp.float32)
    for part, scale in ((jnp.right_shift(slots, 7), 128.0), (jnp.bitwise_and(slots, 127), 1.0)):
        chosen = jnp.where(is_slot, part.astype(jnp.float32), 0.0).astype(jnp.bfloat16)
        ordered += scale * lax.dot_general(
            chosen, is_owner, NT, preferred_element_type=jnp.float32
        )
    place = lax.div(iota((1, wide), 1), waves)
    pieces = []
    for g in range(groups):
        piece = jnp.zeros((1, wide), jnp.float32)
        for k in range(group):
            row = g * group + k
            piece = jnp.where(place == k, ordered[row : row + 1], piece)
        pieces.append(piece)
    order_waves = jnp.concatenate(pieces, axis=1)
    inverse = 1.0 / jnp.full((1, 1), points, jnp.float32)

    def table(count, stride, first):
        steps = (iota((count, total), 0) * stride + first).astype(jnp.float32)
        return sincos(order_waves, steps, points, inverse)

    first = lev * (NLON // levs)
    coarse_cos, coarse_sin = table(BLOCK // FINE, FINE, 0)
    fine_cos, fine_sin = table(FINE, 1, 0)
    for a in range(BLOCK // FINE):
        ca, sa = coarse_cos[a : a + 1], coarse_sin[a : a + 1]
        inner[a * FINE : (a + 1) * FINE, :total] = (ca * fine_cos - sa * fine_sin).astype(jnp.bfloat16)
        inner[a * FINE : (a + 1) * FINE, total:] = (-(sa * fine_cos + ca * fine_sin)).astype(jnp.bfloat16)
    outer_cos, outer_sin = table(-(-blocks // 8) * 8, BLOCK, first)
    weight = jnp.where(order_waves == 0.0, 1.0, 2.0)
    pick_row = iota((lanes, 128), 0)
    pick_pair = jnp.where(pick_row < pairs_dev, 2 * pick_row, 2 * (pick_row - pairs_dev) + 1)
    pick = jnp.where(lax.rem(iota((lanes, 128), 1), lanes) == pick_pair, 1.0, 0.0).astype(jnp.bfloat16)
    arrived_slot = lax.div(iota((waves, 128), 1), lanes)

    for sem in (recv_sem, send_sem):
        all_of_them = recv.at[pl.ds(0, devices - 1)]
        pltpu.make_async_copy(all_of_them, all_of_them, sem).wait()

    reals, imags = [], []
    for v in range(levs):
        parts = []
        for g in range(groups):
            block = recv[v * waves : (v + 1) * waves, :, pl.ds(g * 128, 128)].reshape(waves, 128)
            spread = jnp.concatenate(
                [jnp.where(arrived_slot == k, block, 0.0) for k in range(group)], axis=0
            ).astype(jnp.bfloat16)
            parts.append(lax.dot_general(pick, spread, NT, preferred_element_type=jnp.float32))
        coeffs = jnp.concatenate(parts, axis=1) * weight
        reals.append(coeffs[:pairs_dev])
        imags.append(coeffs[pairs_dev:])
    real = jnp.concatenate(reals, axis=0)
    imag = jnp.concatenate(imags, axis=0)
    pairs = real.shape[0]

    at = iota((pairs, BLOCK), 1) + first
    step = blocks
    for start in range(0, blocks, step):
        turned = []
        for j in range(start, start + step):
            c, s = outer_cos[j : j + 1], outer_sin[j : j + 1]
            turned.append(jnp.concatenate(
                [(real * c - imag * s).astype(jnp.bfloat16), (real * s + imag * c).astype(jnp.bfloat16)],
                axis=1,
            ))
        result = lax.dot_general(
            jnp.concatenate(turned, axis=0), inner[...], NT, preferred_element_type=jnp.float32
        )
        for j in range(start, start + step):
            found = result[(j - start) * pairs : (j - start + 1) * pairs]
            found = jnp.where(at + j * BLOCK < points_int, found, 0.0)
            out_ref[:, j * BLOCK : (j + 1) * BLOCK] = found.astype(jnp.bfloat16)
    if blocks * BLOCK < out_ref.shape[1]:
        rest = out_ref.shape[1] - blocks * BLOCK
        out_ref[:, blocks * BLOCK :] = jnp.zeros((pairs, rest), jnp.bfloat16)


def shards(spectra, legendre, wave_slots, row_cycle):
    waves = lax.axis_size("wave")
    levs = lax.axis_size("lev")
    slots_dev, pairs_dev, _, degrees = spectra.shape
    rows = legendre.shape[1]
    total = slots_dev * waves
    region = NLON // levs
    blocks = min(region // BLOCK, -(-(20 + 4 * (CYCLES - 1)) // BLOCK))
    width = slots_dev * 2 * pairs_dev
    vmem = pl.BlockSpec(memory_space=pltpu.VMEM)
    hbm = pl.BlockSpec(memory_space=pltpu.HBM)
    grid = pl.pallas_call(
        functools.partial(kernel, waves, levs, blocks),
        out_shape=pltpu.VMEM((pairs_dev * levs, region), jnp.bfloat16),
        in_specs=[hbm] * 4,
        out_specs=vmem,
        scratch_shapes=[
            pltpu.SMEM((total,), jnp.int32),
            pltpu.SMEM((waves,), jnp.int32),
            pltpu.VMEM((total,), jnp.int32),
            pltpu.VMEM((slots_dev, pairs_dev, 2, degrees), jnp.bfloat16),
            pltpu.VMEM((slots_dev, rows, degrees), jnp.bfloat16),
            pltpu.VMEM((rows, 1, width), jnp.float32),
            pltpu.VMEM((levs * waves, 1, width), jnp.float32),
            pltpu.VMEM((BLOCK, 2 * total), jnp.bfloat16),
            pltpu.SemaphoreType.DMA((3,)),
            pltpu.SemaphoreType.DMA((2, slots_dev * 2 * pairs_dev // 128)),
            pltpu.SemaphoreType.DMA,
            pltpu.SemaphoreType.DMA,
        ],
        compiler_params=pltpu.CompilerParams(
            collective_id=0, has_side_effects=True, vmem_limit_bytes=60 << 20
        ),
    )(wave_slots, row_cycle, spectra, legendre)
    return grid.reshape(grid.shape[0], 1, region)


def solution(mesh):
    placed = (P("wave", "lev", None, None), P("wave", None, None), P(), P())
    return jax.shard_map(
        shards, mesh=mesh, in_specs=placed, out_specs=P(None, "wave", "lev"), check_vma=False
    )
```
